32 devices in a mesh: video: 4 (over y, x), tm: 8 (over z, core).
Axes of the slice: x: 2, y: 2, z: 4, core: 2. Of those that a mesh axis runs over, the one named last changes fastest.
Arguments:
- bin_grad: bfloat16 [16, 32, 16, 1024], P('video', 'tm'), may hold values from -0.125 to 0.125
- tap_weight: float32 [16, 32, 16, 2], P('video', 'tm'), may hold values from 0.05 to 1
- tap_index: int32 [16, 32, 16, 2], P('video', 'tm'), may hold values from 0 to 1023, as said below
- features: bfloat16 [16, 1024, 1024], P('video', 'tm'), may hold values from -6 to 6
- preact: bfloat16 [16, 1024, 1024], P('video', 'tm'), may hold values from -8 to 8
- filter_second: bfloat16 [3, 1024, 1024], replicated, may hold values from -0.109375 to 0.109375
Outputs:
- first_filter_grad: float32 [1024, 3, 1024], P('tm')
- second_filter_grad: float32 [1024, 3, 1024], P('tm')
The draws below stay inside these ranges and needn't reach their ends.
Inputs may be any that keep to these rules, and one draw needn't show every extreme that they name: `tap_index`: each proposal spans the integer snippets a to a + L for a start a and a length L of 1 or more; the taps of bin b are a + ((2 b + 1) L) // 32 and that snippet plus one. For the proposals held by one device (its 4 videos and 4 proposals of each), at most 64 taps fall into any one block of 128 snippets (snippets 128 * m to 128 * m + 127, taken over its videos together), and exactly 64 into some block.
All inputs are finite; a program needn't handle non-finite values.
Results may differ from the reference program's by a relative error of at most 0.0048.
Values may be sent and summed in bfloat16 or wider, within the bound.
A program may use at most 192 MiB of HBM per device.

```python
import jax
import jax.numpy as jnp
from jax import lax

C = 1024
BINS = 16
TAPS = 2
KERNEL = 3
V_DEV = 4
SNIP_DEV = 128
P_DEV = 4
VIDEOS = 16
SNIPS = 1024
PROPS = 32


def lane_spans(key, busiest, tm_total, lane_props):
    keys = jax.random.split(key, 6)
    peers = jnp.arange(tm_total, dtype=jnp.int32)
    forced = (peers == 0) & (busiest != 0) | (peers == busiest + 1)
    eligible = (peers != busiest) & jnp.logical_not(forced)
    ranking = jax.random.permutation(keys[0], tm_total).astype(jnp.int32)
    priority = jnp.where(forced, 2 * tm_total + peers, jnp.where(eligible, ranking, -1 - peers))
    unused, picked = lax.top_k(priority, lane_props - 1)
    begin = jnp.sort(picked.astype(jnp.int32))
    after = jnp.concatenate([begin[1:], jnp.full((1,), tm_total, jnp.int32)])
    limit = jnp.where(busiest > begin, busiest, tm_total)
    finish = jnp.minimum(after, limit)
    lowest = begin * SNIP_DEV
    span = (finish - begin) * SNIP_DEV
    shape = (lane_props - 1,)
    longest = jax.random.randint(keys[1], shape, 1, span).astype(jnp.int32)
    length = jax.random.randint(keys[2], shape, 1, longest + 1).astype(jnp.int32)
    start = lowest + jax.random.randint(keys[3], shape, 0, span - length).astype(jnp.int32)
    short_len = jax.random.randint(keys[4], (1,), 1, SNIP_DEV).astype(jnp.int32)
    short_start = busiest * SNIP_DEV + jax.random.randint(keys[5], (1,), 0, SNIP_DEV - short_len).astype(jnp.int32)
    return (jnp.concatenate([short_start, start]), jnp.concatenate([short_len, length]))


def device_taps(key, tm_total):
    prop_total = V_DEV * P_DEV
    lane_total = (prop_total + tm_total - 1) // tm_total
    lane_props = prop_total // lane_total
    key_busy, key_lanes, key_mix = jax.random.split(key, 3)
    busiest = jax.random.randint(key_busy, (), 0, tm_total).astype(jnp.int32)
    lane_keys = jax.random.split(key_lanes, lane_total)
    starts, lengths = jax.vmap(lambda single: lane_spans(single, busiest, tm_total, lane_props))(lane_keys)
    order = jax.random.permutation(key_mix, prop_total)
    starts = starts.reshape(prop_total)[order]
    lengths = lengths.reshape(prop_total)[order]
    centre = 2 * jnp.arange(BINS, dtype=jnp.int32) + 1
    first = starts[:, None] + centre[None, :] * lengths[:, None] // (2 * BINS)
    taps = jnp.stack([first, first + 1], axis=-1)
    return taps.reshape(V_DEV, P_DEV, BINS, TAPS).astype(jnp.int32)


def draw_tap_index(key, part):
    key = jax.random.fold_in(key, 7)
    video_total = VIDEOS // V_DEV
    tm_total = PROPS // P_DEV
    keys = jax.random.split(key, video_total * tm_total)
    blocks = jax.vmap(lambda single: device_taps(single, tm_total))(keys)
    blocks = blocks.reshape(video_total, tm_total, V_DEV, P_DEV, BINS, TAPS).transpose(0, 2, 1, 3, 4, 5)
    return blocks.reshape(VIDEOS, PROPS, BINS, TAPS).astype(jnp.int32)


def steps_of(rng, extent, cuts, least, high):
    factor_of = 1.0
    for position, shards_of in cuts:
        draws = jax.random.uniform(jax.random.fold_in(jax.random.fold_in(rng, 6), position), (shards_of,), jnp.float32, least / len(cuts), high / len(cuts))
        factor_of = factor_of * jnp.repeat(jnp.exp(draws), extent[position] // shards_of).reshape((-1,) + (1,) * (len(extent) - 1 - position))
    return factor_of


def scatter_about(stream_key, dims, spread, most, cuts=(), kind=jnp.bfloat16):
    drawn = spread * jax.random.normal(stream_key, dims, jnp.float32)
    if cuts:
        drawn = drawn * steps_of(stream_key, dims, cuts, -0.22, 0.18)
    return jnp.clip(drawn, -most, most).astype(kind)


def setup_inputs(seed: int = 0) -> dict:
    arg_keys = jax.random.split(jax.random.key(seed), 7)
    bin_grad = scatter_about(arg_keys[0], (VIDEOS, PROPS, BINS, C), (3.0 / (VIDEOS * SNIPS) ** 0.5), 0.125, ((0, 4), (1, 8)))
    tap_weight = jnp.clip(0.05 + 0.95 * jax.random.uniform(arg_keys[1], (VIDEOS, PROPS, BINS, TAPS), jnp.float32) ** steps_of(arg_keys[1], (VIDEOS, PROPS, BINS, TAPS), ((0, 4), (1, 8)), -0.2, 0.2), 0.05, 1.0)
    tap_index = draw_tap_index(jax.random.fold_in(arg_keys[6], 71), 0)
    features = scatter_about(arg_keys[3], (VIDEOS, SNIPS, C), 1.0, 6.0, ((0, 4), (1, 8)))
    preact = scatter_about(arg_keys[4], (VIDEOS, SNIPS, C), 1.5, 8.0, ((0, 4), (1, 8)))
    filter_second = scatter_about(arg_keys[5], (KERNEL, C, C), (KERNEL * C) ** -0.5, 0.109375)
    return dict(bin_grad=bin_grad, tap_weight=tap_weight, tap_index=tap_index, features=features, preact=preact, filter_second=filter_second)


def silu_slope(values):
    sigma = jax.nn.sigmoid(values)
    return sigma * (1.0 + values * (1.0 - sigma))

def filter_grad(inputs, gradients):
    padded = jnp.pad(inputs, ((0, 0), (1, 1), (0, 0)))
    blocks = []
    for lag_index in range(KERNEL):
        window = padded[:, lag_index:lag_index + SNIPS, :].reshape(-1, C)
        blocks.append(jnp.dot(window.T, gradients, preferred_element_type=jnp.float32))
    return jnp.stack(blocks, axis=1)

def reference(bin_grad, tap_weight, tap_index, features, preact, filter_second):
    scaled = (tap_weight[..., None] * bin_grad[:, :, :, None, :].astype(jnp.float32)).astype(jnp.bfloat16)
    video_of = lax.broadcasted_iota(jnp.int32, tap_index.shape, 0)
    segment = (video_of * SNIPS + tap_index).reshape(-1).astype(jnp.int32)
    summed = jax.ops.segment_sum(scaled.reshape(-1, C).astype(jnp.float32), segment, num_segments=VIDEOS * SNIPS)
    snippet_grad = summed.astype(jnp.bfloat16).reshape(VIDEOS, SNIPS, C)
    pre_values = preact.astype(jnp.float32)
    activation = jax.nn.silu(pre_values).astype(jnp.bfloat16)
    grad_padded = jnp.pad(snippet_grad, ((0, 0), (1, 1), (0, 0)))
    act_grad = jnp.zeros((VIDEOS * SNIPS, C), jnp.float32)
    for lag_index in range(KERNEL):
        window = grad_padded[:, 2 - lag_index:2 - lag_index + SNIPS, :].reshape(-1, C)
        act_grad = act_grad + jnp.dot(window, filter_second[lag_index].T, preferred_element_type=jnp.float32)
    pre_grad = (act_grad * silu_slope(pre_values.reshape(-1, C))).astype(jnp.bfloat16)
    first = filter_grad(features, pre_grad)
    second = filter_grad(activation, snippet_grad.reshape(-1, C))
    return (first, second)
```

```python
import functools

import jax
import jax.numpy as jnp
from jax import lax
from jax.experimental import pallas as pl
from jax.experimental.pallas import tpu as pltpu
from jax.sharding import PartitionSpec as P

MESH = pl.DeviceIdType.MESH
UNITS = 2


def silu_slope(values):
    sigma = jax.nn.sigmoid(values)
    return sigma * (1.0 + values * (1.0 - sigma))


def reduce_kernel(tm, steps, rows, cols, q_ref, out_ref, r1, s1, r2, t2, r3, g4, r4,
                  p1_s, p1_r, p2_s, p2_r, p3_s, p3_r, p4_s, p4_r):
    depth = tm // 2
    video = lax.axis_index("video")
    here = lax.axis_index("tm")
    x, y = lax.rem(video, 2), video // 2
    core, z = lax.rem(here, 2), here // 2
    flip_x = y * 2 + (1 - x)
    flip_y = (1 - y) * 2 + x
    flip_xy = (1 - y) * 2 + (1 - x)
    others = (flip_x, flip_y, flip_xy)
    other_bits = ((1 - x, y), (x, 1 - y), (1 - x, 1 - y))
    half, quarter = cols // 4, cols // 8

    def z_peer(j):
        return lax.rem(z + 1 + j, depth) * 2 + core

    def z_slot_row(peer_z):
        return pl.multiple_of(peer_z * rows, rows)

    barrier = pltpu.get_barrier_semaphore()
    for v in others:
        pl.semaphore_signal(barrier, inc=1, device_id={"video": v}, device_id_type=MESH)
    for j in range(depth - 1):
        pl.semaphore_signal(barrier, inc=1, device_id={"tm": z_peer(j)}, device_id_type=MESH)
    pl.semaphore_wait(barrier, 3 + depth - 1)

    def bits(kind, xb, yb):
        return (xb, yb) if kind == 0 else (yb, xb)

    def first(step, kind):
        u = step * UNITS + kind
        h1, _ = bits(kind, 1 - x, 1 - y)
        col = pl.multiple_of(kind * (cols // 2) + h1 * half, 128)
        return pltpu.make_async_remote_copy(
            src_ref=q_ref.at[step, :, pl.ds(col, half)], dst_ref=r1.at[u],
            send_sem=p1_s.at[u], recv_sem=p1_r.at[u],
            device_id={"video": (flip_x, flip_y)[kind]}, device_id_type=MESH)

    def second(step, kind):
        u = step * UNITS + kind
        _, h2 = bits(kind, 1 - x, 1 - y)
        return pltpu.make_async_remote_copy(
            src_ref=s1.at[u, :, pl.ds(pl.multiple_of(h2 * quarter, 128), quarter)], dst_ref=r2.at[u],
            send_sem=p2_s.at[u], recv_sem=p2_r.at[u],
            device_id={"video": (flip_y, flip_x)[kind]}, device_id_type=MESH)

    def third(step, kind, j):
        u = step * UNITS + kind
        peer = lax.rem(z + 1 + j, depth)
        return pltpu.make_async_remote_copy(
            src_ref=t2.at[u, pl.ds(z_slot_row(peer), rows)], dst_ref=r3.at[u, j],
            send_sem=p3_s.at[u, j], recv_sem=p3_r.at[u, j],
            device_id={"tm": peer * 2 + core}, device_id_type=MESH)

    def fourth(step, kind, j):
        u = step * UNITS + kind
        return pltpu.make_async_remote_copy(
            src_ref=g4.at[u], dst_ref=r4.at[u, j],
            send_sem=p4_s.at[u, j], recv_sem=p4_r.at[u, j],
            device_id={"video": others[j]}, device_id_type=MESH)

    def column(kind, xb, yb):
        h1, h2 = bits(kind, xb, yb)
        return pl.ds(pl.multiple_of(kind * (cols // 2) + h1 * half + h2 * quarter, 128), quarter)

    for step in range(min(2, steps)):
        for kind in range(UNITS):
            first(step, kind).start()

    for turn in range(steps + 3):
        if turn + 2 < steps:
            for kind in range(UNITS):
                first(turn + 2, kind).start()
        if turn < steps:
            for kind in range(UNITS):
                u = turn * UNITS + kind
                first(turn, kind).wait_recv()
                h1, _ = bits(kind, x, y)
                col = pl.multiple_of(kind * (cols // 2) + h1 * half, 128)
                s1[u] = (q_ref[turn, :, pl.ds(col, half)].astype(jnp.float32)
                         + r1[u].astype(jnp.float32)).astype(jnp.bfloat16)
                second(turn, kind).start()
        step = turn - 1
        if 0 <= step < steps:
            for kind in range(UNITS):
                u = step * UNITS + kind
                second(step, kind).wait_recv()
                _, h2 = bits(kind, x, y)
                mine = s1[u, :, pl.ds(pl.multiple_of(h2 * quarter, 128), quarter)]
                t2[u] = (mine.astype(jnp.float32) + r2[u].astype(jnp.float32)).astype(jnp.bfloat16)
                for j in range(depth - 1):
                    third(step, kind, j).start()
        step = turn - 2
        if 0 <= step < steps:
            for kind in range(UNITS):
                u = step * UNITS + kind
                total = t2[u, pl.ds(z_slot_row(z), rows)].astype(jnp.float32)
                for j in range(depth - 1):
                    third(step, kind, j).wait_recv()
                    total = total + r3[u, j].astype(jnp.float32)
                g4[u] = total.astype(jnp.bfloat16)
                for j in range(3):
                    fourth(step, kind, j).start()
                out_ref[step, :, column(kind, x, y)] = g4[u].astype(jnp.float32)
        step = turn - 3
        if 0 <= step < steps:
            for kind in range(UNITS):
                u = step * UNITS + kind
                for j in range(3):
                    fourth(step, kind, j).wait_recv()
                    out_ref[step, :, column(kind, *other_bits[j])] = r4[u, j].astype(jnp.float32)

    for step in range(steps):
        for kind in range(UNITS):
            first(step, kind).wait_send()
            second(step, kind).wait_send()
            for j in range(depth - 1):
                third(step, kind, j).wait_send()
            for j in range(3):
                fourth(step, kind, j).wait_send()


def reduce_all(partials):
    steps, chip_rows, cols = partials.shape
    tm = lax.axis_size("tm")
    depth = tm // 2
    rows = chip_rows // depth
    n = steps * UNITS
    half, quarter = cols // 4, cols // 8
    bf = jnp.bfloat16
    dma = pltpu.SemaphoreType.DMA
    vmem = pl.BlockSpec(memory_space=pltpu.VMEM)
    return pl.pallas_call(
        functools.partial(reduce_kernel, tm, steps, rows, cols),
        out_shape=jax.ShapeDtypeStruct((steps, rows, cols), jnp.float32),
        in_specs=[vmem],
        out_specs=vmem,
        scratch_shapes=[
            pltpu.VMEM((n, chip_rows, half), bf),
            pltpu.VMEM((n, chip_rows, half), bf),
            pltpu.VMEM((n, chip_rows, quarter), bf),
            pltpu.VMEM((n, chip_rows, quarter), bf),
            pltpu.VMEM((n, depth - 1, rows, quarter), bf),
            pltpu.VMEM((n, rows, quarter), bf),
            pltpu.VMEM((n, 3, rows, quarter), bf),
            dma((n,)), dma((n,)), dma((n,)), dma((n,)),
            dma((n, depth - 1)), dma((n, depth - 1)), dma((n, 3)), dma((n, 3)),
        ],
        compiler_params=pltpu.CompilerParams(
            collective_id=0, has_side_effects=True, vmem_limit_bytes=48 * 1024 * 1024
        ),
        name="reduce_filters",
    )(partials)


def shifts(count, by):
    up = [(i, i + by) for i in range(count - by)]
    return up, [(j, i) for i, j in up]


def on_device(bin_grad, tap_weight, tap_index, features, preact, filter_second):
    video_count, prop_count, bin_count, tap_count = tap_index.shape
    snip_count = features.shape[1]
    channels = features.shape[2]
    peers = lax.axis_size("tm")
    depth = peers // 2
    rows = channels // peers
    core = lax.rem(lax.axis_index("tm"), 2)
    unit_count = video_count * prop_count * bin_count * tap_count
    capacity = bin_count * tap_count * ((video_count * prop_count + peers - 1) // peers)
    siblings = [(i, i + 1 - 2 * (i % 2)) for i in range(peers)]

    def chip_rows_of(mine, other):
        got = lax.ppermute(other, "tm", siblings)
        return jnp.concatenate(
            [jnp.where(core == 0, mine, got), jnp.where(core == 0, got, mine)], axis=1
        )

    def chip_lhs(values):
        split = values.reshape(video_count, snip_count, depth, 2, rows)
        pick = lambda c: lax.dynamic_index_in_dim(split, c, 3, keepdims=False).reshape(
            video_count, snip_count, depth * rows
        )
        return chip_rows_of(pick(core), pick(1 - core))

    pre_values = preact.astype(jnp.float32)
    activation = jax.nn.silu(pre_values).astype(jnp.bfloat16)
    lhs = jnp.stack([chip_lhs(features), chip_lhs(activation)])
    up, down = shifts(peers, 2)
    before = lax.ppermute(lhs[:, :, -1:], "tm", up)
    after = lax.ppermute(lhs[:, :, :1], "tm", down)
    lhs = jnp.concatenate([before, lhs, after], axis=2)

    scaled = tap_weight[..., None] * bin_grad[:, :, :, None, :].astype(jnp.float32)
    tap_rows = scaled.astype(jnp.bfloat16).reshape(unit_count, channels)
    target = (tap_index // snip_count).reshape(unit_count)
    video_of = lax.broadcasted_iota(jnp.int32, tap_index.shape, 0)
    local_row = (video_of * snip_count + tap_index % snip_count).reshape(unit_count)
    peer_hits = (target[:, None] == jnp.arange(peers, dtype=jnp.int32)[None, :]).astype(jnp.int32)
    earlier = jnp.cumsum(peer_hits, axis=0) - peer_hits
    position = jnp.sum(earlier * peer_hits, axis=1)
    slot_index = target * capacity + position
    matches = slot_index[None, :] == jnp.arange(peers * capacity, dtype=jnp.int32)[:, None]
    send_rows = jnp.dot(
        matches.astype(jnp.bfloat16), tap_rows, preferred_element_type=jnp.float32
    ).astype(jnp.bfloat16)
    send_index = jnp.max(jnp.where(matches, local_row[None, :], -1), axis=1)
    got_rows, got_index = (
        lax.all_to_all(
            send_rows.reshape(peers, capacity, channels),
            "tm",
            split_axis=0,
            concat_axis=0,
            tiled=True,
        ),
        lax.all_to_all(
            send_index.reshape(peers, capacity), "tm", split_axis=0, concat_axis=0, tiled=True
        ),
    )
    gather_table = (
        got_index.reshape(1, -1) == jnp.arange(video_count * snip_count, dtype=jnp.int32)[:, None]
    ).astype(jnp.bfloat16)
    snippet_grad = jnp.dot(
        gather_table, got_rows.reshape(-1, channels), preferred_element_type=jnp.float32
    ).astype(jnp.bfloat16).reshape(video_count, snip_count, channels)

    up, down = shifts(peers, 1)
    grad_before = lax.ppermute(snippet_grad[:, -1:], "tm", up)
    grad_after = lax.ppermute(snippet_grad[:, :1], "tm", down)
    grad_padded = jnp.concatenate([grad_before, snippet_grad, grad_after], axis=1)

    def filter_terms(padded, gradients):
        gradients = gradients.reshape(-1, channels)
        return [
            lax.dot_general(
                padded[:, k : k + 2 * snip_count].reshape(-1, depth * rows), gradients,
                (((0,), (0,)), ((), ())), preferred_element_type=jnp.float32,
            ).astype(jnp.bfloat16)
            for k in range(3)
        ]

    second_terms = filter_terms(lhs[1], chip_rows_of(snippet_grad, snippet_grad))
    act_grad = jnp.zeros((video_count * snip_count, channels), jnp.float32)
    for lag_index in range(3):
        window = grad_padded[:, 2 - lag_index : 2 - lag_index + snip_count, :].reshape(-1, channels)
        act_grad = act_grad + lax.dot_general(
            window,
            filter_second[lag_index],
            (((1,), (1,)), ((), ())),
            preferred_element_type=jnp.float32,
        )
    pre_grad = (act_grad * silu_slope(pre_values.reshape(-1, channels))).astype(jnp.bfloat16)
    pre_grad = pre_grad.reshape(video_count, snip_count, channels)
    first_terms = filter_terms(lhs[0], chip_rows_of(pre_grad, pre_grad))
    sums = reduce_all(jnp.stack(second_terms + first_terms))
    out = sums.reshape(2, 3, rows, channels).transpose(0, 2, 1, 3)
    return (out[1], out[0])


def solution(mesh):
    return jax.shard_map(
        on_device,
        mesh=mesh,
        in_specs=(
            P("video", "tm", None, None),
            P("video", "tm", None, None),
            P("video", "tm", None, None),
            P("video", "tm", None),
            P("video", "tm", None),
            P(),
        ),
        out_specs=(P("tm", None, None), P("tm", None, None)),
        check_vma=False,
    )
```

```python
import functools

import jax
import jax.numpy as jnp
from jax import lax
from jax.experimental import pallas as pl
from jax.experimental.pallas import tpu as pltpu
from jax.sharding import PartitionSpec as P

MESH = pl.DeviceIdType.MESH
UNITS = 2
VMEM_LIMIT = 60 * 1024 * 1024


def silu_slope(values):
    sigma = jax.nn.sigmoid(values)
    return sigma * (1.0 + values * (1.0 - sigma))


def row_of(ref, index, *lead):
    group = ref[(*lead, pl.ds(index // 16 * 16, 16), slice(None))].astype(jnp.float32)
    return group[index % 16 : index % 16 + 1, :]


def pack_rows(row_list):
    width = row_list[0].shape[1]
    place = lax.broadcasted_iota(jnp.int32, (16, width), 0)
    packed = jnp.zeros((16, width), jnp.float32)
    for i, row in enumerate(row_list):
        packed = jnp.where(place == i, row, packed)
    return packed.astype(jnp.bfloat16)


def moved(block, edge, amount):
    count = block.shape[0]
    place = lax.broadcasted_iota(jnp.int32, block.shape, 0)
    if amount == 1:
        return jnp.where(place == 0, edge, pltpu.roll(block, 1, 0))
    return jnp.where(place == count - 1, edge, pltpu.roll(block, count - 1, 0))


def whole_kernel(tm, steps, rows, cols, videos, snips, cap, bin_ref, weight_ref, index_ref, feat_ref,
                 pre_ref, pre_lhs_ref, filt_hbm, out_ref, filt, tap_rows, srow, sidx, grow, gidx, act, lhs, win,
                 edge_out, edge_in, gs, gp, gmove, gedge_out, gedge_in, acc, q_ref,
                 r1, s1, r2, t2, r3, g4, r4,
                 p1_s, p1_r, p2_s, p2_r, p3_s, p3_r, p4_s, p4_r,
                 row_s, row_r, idx_s, idx_r, lhs_s, lhs_r, edge_s, edge_r, g_s, g_r, ge_s, ge_r, filt_sem):
    depth = tm // 2
    bf, f32 = jnp.bfloat16, jnp.float32
    own = videos * snips
    bins = bin_ref.shape[0]
    taps = 2 * bins
    chip = depth * rows
    aligned = rows % 128 == 0
    pack = 128 // cap
    blocks = depth if aligned else 1
    width = chip // blocks
    video = lax.axis_index("video")
    here = lax.axis_index("tm")
    x, y = lax.rem(video, 2), video // 2
    core, z = lax.rem(here, 2), here // 2
    sibling = z * 2 + 1 - core
    flip_x = y * 2 + (1 - x)
    flip_y = (1 - y) * 2 + x
    flip_xy = (1 - y) * 2 + (1 - x)
    others = (flip_x, flip_y, flip_xy)
    other_bits = ((1 - x, y), (x, 1 - y), (1 - x, 1 - y))
    half, quarter = cols // 4, cols // 8

    def z_slot_row(peer_z):
        return pl.multiple_of(peer_z * rows, rows)

    filt_copy = pltpu.make_async_copy(filt_hbm, filt, filt_sem)
    filt_copy.start()
    barrier = pltpu.get_barrier_semaphore()
    for v in others:
        pl.semaphore_signal(barrier, inc=1, device_id={"video": v}, device_id_type=MESH)

    @pl.loop(1, tm)
    def _(j):
        pl.semaphore_signal(barrier, inc=1, device_id={"tm": lax.rem(here + j, tm)}, device_id_type=MESH)

    for j in range(2):
        tap_rows[j * bins : (j + 1) * bins, :] = (
            weight_ref[:, j : j + 1] * bin_ref[...].astype(f32)).astype(bf)
    index = index_ref[...]
    target = index // snips
    lane = lax.broadcasted_iota(jnp.int32, (1, taps), 1)
    video_of = lax.rem(lane, bins) // (bins // videos)
    place8 = lax.broadcasted_iota(jnp.int32, (tm, taps), 0)
    hits = (place8 == target).astype(f32)
    upper = (lax.broadcasted_iota(jnp.int32, (taps, taps), 0)
             < lax.broadcasted_iota(jnp.int32, (taps, taps), 1)).astype(f32).astype(bf)
    earlier = jnp.dot(hits.astype(bf), upper, preferred_element_type=f32)
    position = jnp.sum(earlier * hits, axis=0, keepdims=True).astype(jnp.int32)
    slot = target * cap + position
    group = min(512, tm * cap)
    for g in range(tm * cap // group):
        match = (slot - g * group == lax.broadcasted_iota(jnp.int32, (group, taps), 0)).astype(f32).astype(bf)
        srow[g * group : (g + 1) * group, :] = jnp.dot(
            match, tap_rows[...], preferred_element_type=f32).astype(bf)
    place = lax.broadcasted_iota(jnp.int32, (8, taps), 0)
    coded = jnp.where(place == 0, (video_of + 1).astype(f32), 0.0)
    coded = jnp.where(place == 1, (index - target * snips).astype(f32), coded).astype(bf)

    @pl.loop(0, tm)
    def _(d):
        offset = lax.rem(lax.rem(d - here + tm, tm), pack) * cap
        wide = (target - d) * 4096 + position + offset
        match = (wide == lax.broadcasted_iota(jnp.int32, (128, taps), 0)).astype(f32).astype(bf)
        sidx[d] = lax.dot_general(coded, match, (((1,), (1,)), ((), ())), preferred_element_type=f32)

    def row_copy(j):
        peer = lax.rem(here + j, tm)
        return pltpu.make_async_remote_copy(
            src_ref=srow.at[pl.ds(pl.multiple_of(peer * cap, cap), cap)], dst_ref=grow.at[j],
            send_sem=row_s.at[j], recv_sem=row_r.at[j], device_id={"tm": peer}, device_id_type=MESH)

    def idx_copy(j):
        peer = lax.rem(here + j, tm)
        return pltpu.make_async_remote_copy(
            src_ref=sidx.at[peer], dst_ref=gidx.at[j],
            send_sem=idx_s.at[j], recv_sem=idx_r.at[j], device_id={"tm": peer}, device_id_type=MESH)

    grow[0] = srow[pl.ds(pl.multiple_of(here * cap, cap), cap), :]
    gidx[0] = sidx[here]
    pl.semaphore_wait(barrier, 3 + tm - 1)

    @pl.loop(1, tm)
    def _(j):
        idx_copy(j).start()
        row_copy(j).start()

    def column_of(b, c):
        start = (b * 2 + c) * rows if aligned else c * chip
        return pl.ds(pl.multiple_of(start, 128), width)

    def lhs_copy(kind, b):
        source = (feat_ref, act)[kind]
        return pltpu.make_async_remote_copy(
            src_ref=source.at[:, column_of(b, 1 - core)],
            dst_ref=lhs.at[kind, core, :, pl.ds(b * width, width)],
            send_sem=lhs_s.at[kind, b], recv_sem=lhs_r.at[kind, b],
            device_id={"tm": sibling}, device_id_type=MESH)

    for b in range(blocks):
        lhs_copy(0, b).start()

    @pl.loop(0, own // 64)
    def _(r):
        part = pl.ds(pl.multiple_of(r * 64, 64), 64)
        values = pre_lhs_ref[part, :].astype(f32)
        act[part, :] = (values * jax.nn.sigmoid(values)).astype(bf)

    for b in range(blocks):
        lhs_copy(1, b).start()
    for side in range(2):
        at = 0 if side == 0 else snips - 1
        edge_out[side] = pack_rows(
            [row_of(ref, v * snips + at) for ref in (feat_ref, act) for v in range(videos)])
    toward = lax.rem(z + 2 * core - 1 + depth, depth)

    def edge_copy(c):
        return pltpu.make_async_remote_copy(
            src_ref=edge_out.at[core], dst_ref=edge_in.at[1 - core],
            send_sem=edge_s.at[c], recv_sem=edge_r.at[1 - core],
            device_id={"tm": toward * 2 + c}, device_id_type=MESH)

    def edge_arrival(s):
        return pltpu.make_async_remote_copy(
            src_ref=edge_out.at[0], dst_ref=edge_in.at[s],
            send_sem=edge_s.at[0], recv_sem=edge_r.at[s],
            device_id={"tm": sibling}, device_id_type=MESH)

    for c in range(2):
        edge_copy(c).start()
    for kind in range(2):
        for b in range(blocks):
            lhs[kind, core, :, b * width : (b + 1) * width] = (feat_ref, act)[kind][:, column_of(b, core)]
    for s in range(2):
        edge_arrival(s).wait_recv()
    for kind in range(2):
        for b in range(blocks):
            lhs_copy(kind, b).wait_recv()
        for b in range(blocks):
            piece = pl.ds(b * width, width)
            for v in range(videos):
                spot = kind * videos + v
                halves = [lhs[kind, c, v * snips : (v + 1) * snips, piece].astype(f32) for c in range(2)]
                ends = [jnp.where(edge_ok, edge_in[s, :, column_of(b, core)].astype(f32)[spot : spot + 1, :], 0.0)
                        for s, edge_ok in ((0, z > 0), (1, z < depth - 1))]
                for c in range(2):
                    span = pl.ds(c * own + v * snips, snips)
                    prior = ends[0] if c == 0 else halves[0][snips - 1 :, :]
                    later = ends[1] if c == 1 else halves[1][:1, :]
                    win[kind, 0, piece, span] = moved(halves[c], prior, 1).T.astype(bf)
                    win[kind, 1, piece, span] = halves[c].T.astype(bf)
                    win[kind, 2, piece, span] = moved(halves[c], later, -1).T.astype(bf)

    @pl.loop(1, tm)
    def _(j):
        idx_copy(j).wait_recv()
        row_copy(j).wait_recv()

    many = min(8, tm)
    chunk = 256
    for g in range(tm // many):
        pieces = []
        for j in range(g * many, (g + 1) * many, pack):
            both = gidx[j]
            for i in range(1, pack):
                both = both + gidx[j + i]
            code = both[0:1, :] * float(snips) + both[1:2, :] - float(snips)
            spots = lax.broadcasted_iota(jnp.int32, (own, 128), 0).astype(f32)
            pieces.append((spots == code).astype(f32).astype(bf))
        table = jnp.concatenate(pieces, axis=1)
        for n in range(cols // chunk):
            part = slice(n * chunk, (n + 1) * chunk)
            term = jnp.dot(table, grow[g * many : (g + 1) * many, :, part].reshape(many * cap, chunk),
                           preferred_element_type=f32)
            if tm == many:
                gs[core, :, part] = term.astype(bf)
            else:
                acc[:, part] = term if g == 0 else acc[:, part] + term
    if tm != many:
        gs[core] = acc[...].astype(bf)

    def grad_copy(i):
        ref = (gs, gp)[i]
        return pltpu.make_async_remote_copy(
            src_ref=ref.at[core], dst_ref=ref.at[core],
            send_sem=g_s.at[i], recv_sem=g_r.at[i], device_id={"tm": sibling}, device_id_type=MESH)

    grad_copy(0).start()
    gedge_out[...] = pack_rows([
        jnp.where(core == 1, row_of(gs, v * snips + snips - 1, core), row_of(gs, v * snips, core))
        for v in range(videos)])
    gedge_copy = pltpu.make_async_remote_copy(
        src_ref=gedge_out, dst_ref=gedge_in, send_sem=ge_s, recv_sem=ge_r,
        device_id={"tm": toward * 2 + 1 - core}, device_id_type=MESH)
    gedge_copy.start()

    def product(step):
        kind, k = (1, step) if step < 3 else (0, step - 3)
        grads = gs if step < 3 else gp

        @pl.loop(0, cols // chunk)
        def _(n):
            part = pl.ds(pl.multiple_of(n * chunk, chunk), chunk)
            q_ref[step, :, part] = jnp.dot(
                win[kind, k], grads[:, :, part].reshape(2 * own, chunk), preferred_element_type=f32).astype(bf)

    def bits(kind, xb, yb):
        return (xb, yb) if kind == 0 else (yb, xb)

    def first(step, kind):
        u = step * UNITS + kind
        h1, _ = bits(kind, 1 - x, 1 - y)
        col = pl.multiple_of(kind * (cols // 2) + h1 * half, 128)
        return pltpu.make_async_remote_copy(
            src_ref=q_ref.at[step, :, pl.ds(col, half)], dst_ref=r1.at[u],
            send_sem=p1_s.at[u], recv_sem=p1_r.at[u],
            device_id={"video": (flip_x, flip_y)[kind]}, device_id_type=MESH)

    def second(step, kind):
        u = step * UNITS + kind
        _, h2 = bits(kind, 1 - x, 1 - y)
        return pltpu.make_async_remote_copy(
            src_ref=s1.at[u, :, pl.ds(pl.multiple_of(h2 * quarter, 128), quarter)], dst_ref=r2.at[u],
            send_sem=p2_s.at[u], recv_sem=p2_r.at[u],
            device_id={"video": (flip_y, flip_x)[kind]}, device_id_type=MESH)

    def third(step, kind, j):
        u = step * UNITS + kind
        peer = lax.rem(z + 1 + j, depth)
        return pltpu.make_async_remote_copy(
            src_ref=t2.at[u, pl.ds(z_slot_row(peer), rows)], dst_ref=r3.at[u, j],
            send_sem=p3_s.at[u, j], recv_sem=p3_r.at[u, j],
            device_id={"tm": peer * 2 + core}, device_id_type=MESH)

    def fourth(step, kind, j):
        u = step * UNITS + kind
        return pltpu.make_async_remote_copy(
            src_ref=g4.at[u], dst_ref=r4.at[u, j],
            send_sem=p4_s.at[u, j], recv_sem=p4_r.at[u, j],
            device_id={"video": others[j]}, device_id_type=MESH)

    def column(kind, xb, yb):
        h1, h2 = bits(kind, xb, yb)
        return pl.ds(pl.multiple_of(kind * (cols // 2) + h1 * half + h2 * quarter, 128), quarter)


    def ready(step):
        if step == 3:
            grad_copy(1).wait_recv()
        product(step)
        for kind in range(UNITS):
            first(step, kind).start()

    grad_copy(0).wait_recv()
    ready(0)

    gedge_copy.wait_recv()
    outside_ok = jnp.where(core == 1, z < depth - 1, z > 0)
    outside = jnp.where(outside_ok, gedge_in[...].astype(f32), 0.0)
    for v in range(videos):
        mine = gs[core, v * snips : (v + 1) * snips, :].astype(f32)
        far = outside[v : v + 1, :]
        near = jnp.where(core == 1, row_of(gs, v * snips + snips - 1, 1 - core), row_of(gs, v * snips, 1 - core))
        prior = jnp.where(core == 1, near, far)
        later = jnp.where(core == 1, far, near)
        gmove[0, v * snips : (v + 1) * snips, :] = moved(mine, prior, 1).astype(bf)
        gmove[1, v * snips : (v + 1) * snips, :] = moved(mine, later, -1).astype(bf)
    filt_copy.wait()

    @pl.loop(0, cols // chunk)
    def _(n):
        part = pl.ds(pl.multiple_of(n * chunk, chunk), chunk)
        total = jnp.zeros((own, chunk), f32)
        for lag, window in enumerate((gmove[1], gs[core], gmove[0])):
            total = total + lax.dot_general(
                window, filt[lag, part, :], (((1,), (1,)), ((), ())), preferred_element_type=f32)
        gp[core, :, part] = (total * silu_slope(pre_ref[:, part].astype(f32))).astype(bf)

    grad_copy(1).start()
    ready(1)

    for turn in range(steps + 3):
        if turn + 2 < steps:
            ready(turn + 2)
        if turn < steps:
            for kind in range(UNITS):
                u = turn * UNITS + kind
                first(turn, kind).wait_recv()
                h1, _ = bits(kind, x, y)
                col = pl.multiple_of(kind * (cols // 2) + h1 * half, 128)
                s1[u] = (q_ref[turn, :, pl.ds(col, half)].astype(jnp.float32)
                         + r1[u].astype(jnp.float32)).astype(jnp.bfloat16)
                second(turn, kind).start()
        step = turn - 1
        if 0 <= step < steps:
            for kind in range(UNITS):
                u = step * UNITS + kind
                second(step, kind).wait_recv()
                _, h2 = bits(kind, x, y)
                mine = s1[u, :, pl.ds(pl.multiple_of(h2 * quarter, 128), quarter)]
                t2[u] = (mine.astype(jnp.float32) + r2[u].astype(jnp.float32)).astype(jnp.bfloat16)
                for j in range(depth - 1):
                    third(step, kind, j).start()
        step = turn - 2
        if 0 <= step < steps:
            for kind in range(UNITS):
                u = step * UNITS + kind
                total = t2[u, pl.ds(z_slot_row(z), rows)].astype(jnp.float32)
                for j in range(depth - 1):
                    third(step, kind, j).wait_recv()
                    total = total + r3[u, j].astype(jnp.float32)
                g4[u] = total.astype(jnp.bfloat16)
                for j in range(3):
                    fourth(step, kind, j).start()
                out_ref[step, :, column(kind, x, y)] = g4[u].astype(jnp.float32)
        step = turn - 3
        if 0 <= step < steps:
            for kind in range(UNITS):
                u = step * UNITS + kind
                for j in range(3):
                    fourth(step, kind, j).wait_recv()
                    out_ref[step, :, column(kind, *other_bits[j])] = r4[u, j].astype(jnp.float32)

    for step in range(steps):
        for kind in range(UNITS):
            first(step, kind).wait_send()
            second(step, kind).wait_send()
            for j in range(depth - 1):
                third(step, kind, j).wait_send()
            for j in range(3):
                fourth(step, kind, j).wait_send()
    for c in range(2):
        edge_copy(c).wait_send()
    for kind in range(2):
        for b in range(blocks):
            lhs_copy(kind, b).wait_send()
    for i in range(2):
        grad_copy(i).wait_send()
    gedge_copy.wait_send()

    @pl.loop(1, tm)
    def _(j):
        idx_copy(j).wait_send()
        row_copy(j).wait_send()


def on_device(bin_grad, tap_weight, tap_index, features, preact, filter_second):
    video_count, prop_count, bin_count, tap_count = tap_index.shape
    snips, cols = features.shape[1:]
    tm = lax.axis_size("tm")
    depth = tm // 2
    rows = cols // tm
    chip = depth * rows
    own = video_count * snips
    bins = video_count * prop_count * bin_count
    cap = bin_count * tap_count * ((video_count * prop_count + tm - 1) // tm)
    steps = 6
    n = steps * UNITS
    half, quarter = cols // 4, cols // 8
    blocks = depth if rows % 128 == 0 else 1
    bf, f32 = jnp.bfloat16, jnp.float32
    dma = pltpu.SemaphoreType.DMA
    vmem = pl.BlockSpec(memory_space=pltpu.VMEM)
    features = features.reshape(own, cols)
    preact = preact.reshape(own, cols)

    def by_core(values):
        if rows % 128 == 0:
            return values
        return values.reshape(own, depth, 2, rows).swapaxes(1, 2).reshape(own, cols)

    sums = pl.pallas_call(
        functools.partial(whole_kernel, tm, steps, rows, cols, video_count, snips, cap),
        out_shape=jax.ShapeDtypeStruct((steps, rows, cols), f32),
        in_specs=[vmem] * 6 + [pl.BlockSpec(memory_space=pl.ANY)],
        out_specs=vmem,
        scratch_shapes=[
            pltpu.VMEM(filter_second.shape, bf),
            pltpu.VMEM((2 * bins, cols), bf),
            pltpu.VMEM((tm * cap, cols), bf),
            pltpu.VMEM((tm, 8, 128), f32),
            pltpu.VMEM((tm, cap, cols), bf),
            pltpu.VMEM((tm, 8, 128), f32),
            pltpu.VMEM((own, cols), bf),
            pltpu.VMEM((2, 2, own, chip), bf),
            pltpu.VMEM((2, 3, chip, 2 * own), bf),
            pltpu.VMEM((2, 16, cols), bf),
            pltpu.VMEM((2, 16, cols), bf),
            pltpu.VMEM((2, own, cols), bf),
            pltpu.VMEM((2, own, cols), bf),
            pltpu.VMEM((2, own, cols), bf),
            pltpu.VMEM((16, cols), bf),
            pltpu.VMEM((16, cols), bf),
            pltpu.VMEM((own, cols) if tm > 8 else (8, 128), f32),
            pltpu.VMEM((steps, chip, cols), bf),
            pltpu.VMEM((n, chip, half), bf),
            pltpu.VMEM((n, chip, half), bf),
            pltpu.VMEM((n, chip, quarter), bf),
            pltpu.VMEM((n, chip, quarter), bf),
            pltpu.VMEM((n, depth - 1, rows, quarter), bf),
            pltpu.VMEM((n, rows, quarter), bf),
            pltpu.VMEM((n, 3, rows, quarter), bf),
            dma((n,)), dma((n,)), dma((n,)), dma((n,)),
            dma((n, depth - 1)), dma((n, depth - 1)), dma((n, 3)), dma((n, 3)),
            dma((tm,)), dma((tm,)), dma((tm,)), dma((tm,)),
            dma((2, blocks)), dma((2, blocks)), dma((2,)), dma((2,)),
            dma((2,)), dma((2,)), dma, dma, dma,
        ],
        compiler_params=pltpu.CompilerParams(
            collective_id=0, has_side_effects=True, vmem_limit_bytes=VMEM_LIMIT
        ),
        name="filter_grads",
    )(
        bin_grad.reshape(bins, cols),
        tap_weight.reshape(bins, tap_count),
        tap_index.reshape(bins, tap_count).T.reshape(1, tap_count * bins),
        by_core(features),
        preact,
        by_core(preact),
        filter_second,
    )
    out = sums.reshape(2, 3, rows, cols).transpose(0, 2, 1, 3)
    return (out[1], out[0])


def solution(mesh):
    return jax.shard_map(
        on_device,
        mesh=mesh,
        in_specs=(
            P("video", "tm", None, None),
            P("video", "tm", None, None),
            P("video", "tm", None, None),
            P("video", "tm", None),
            P("video", "tm", None),
            P(),
        ),
        out_specs=(P("tm", None, None), P("tm", None, None)),
        check_vma=False,
    )
```

```python
import functools

import jax
import jax.numpy as jnp
from jax import lax
from jax.experimental import pallas as pl
from jax.experimental.pallas import tpu as pltpu
from jax.sharding import PartitionSpec as P

MESH = pl.DeviceIdType.MESH
UNITS = 2
VMEM_LIMIT = 60 * 1024 * 1024


def silu_slope(values):
    sigma = jax.nn.sigmoid(values)
    return sigma * (1.0 + values * (1.0 - sigma))


def row_of(ref, index, *lead):
    group = ref[(*lead, pl.ds(index // 16 * 16, 16), slice(None))].astype(jnp.float32)
    return group[index % 16 : index % 16 + 1, :]


def pack_rows(row_list):
    width = row_list[0].shape[1]
    place = lax.broadcasted_iota(jnp.int32, (16, width), 0)
    packed = jnp.zeros((16, width), jnp.float32)
    for i, row in enumerate(row_list):
        packed = jnp.where(place == i, row, packed)
    return packed.astype(jnp.bfloat16)


def moved(block, edge, amount):
    count = block.shape[0]
    place = lax.broadcasted_iota(jnp.int32, block.shape, 0)
    if amount == 1:
        return jnp.where(place == 0, edge, pltpu.roll(block, 1, 0))
    return jnp.where(place == count - 1, edge, pltpu.roll(block, count - 1, 0))


def whole_kernel(tm, steps, rows, cols, videos, snips, cap, bin_ref, weight_ref, index_ref, feat_ref,
                 pre_ref, pre_lhs_ref, filt_hbm, out_ref, filt, tap_rows, srow, sidx, grow, gidx, act, lhs, win,
                 edge_out, edge_in, gs, gp, gmove, gedge_out, gedge_in, acc, q_ref,
                 r1, s1, r2, t2, r3, rz, zs, z_s, z_r,
                 p1_s, p1_r, p2_s, p2_r, p3_s, p3_r, p4_s, p4_r,
                 row_s, row_r, idx_s, idx_r, lhs_s, lhs_r, edge_s, edge_r, g_s, g_r, ge_s, ge_r, filt_sem):
    depth = tm // 2
    bf, f32 = jnp.bfloat16, jnp.float32
    own = videos * snips
    bins = bin_ref.shape[0]
    taps = 2 * bins
    chip = depth * rows
    aligned = rows % 128 == 0
    pack = 128 // cap
    blocks = depth if aligned else 1
    width = chip // blocks
    video = lax.axis_index("video")
    here = lax.axis_index("tm")
    x, y = lax.rem(video, 2), video // 2
    core, z = lax.rem(here, 2), here // 2
    sibling = z * 2 + 1 - core
    flip_x = y * 2 + (1 - x)
    flip_y = (1 - y) * 2 + x
    flip_xy = (1 - y) * 2 + (1 - x)
    others = (flip_x, flip_y, flip_xy)
    half, quarter = cols // 4, cols // 8

    def z_slot_row(peer_z):
        return pl.multiple_of(peer_z * rows, rows)

    filt_copy = pltpu.make_async_copy(filt_hbm, filt, filt_sem)
    filt_copy.start()
    barrier = pltpu.get_barrier_semaphore()
    for v in others:
        pl.semaphore_signal(barrier, inc=1, device_id={"video": v}, device_id_type=MESH)

    @pl.loop(1, tm)
    def _(j):
        pl.semaphore_signal(barrier, inc=1, device_id={"tm": lax.rem(here + j, tm)}, device_id_type=MESH)

    for j in range(2):
        tap_rows[j * bins : (j + 1) * bins, :] = (
            weight_ref[:, j : j + 1] * bin_ref[...].astype(f32)).astype(bf)
    index = index_ref[...]
    target = index // snips
    lane = lax.broadcasted_iota(jnp.int32, (1, taps), 1)
    video_of = lax.rem(lane, bins) // (bins // videos)
    place8 = lax.broadcasted_iota(jnp.int32, (tm, taps), 0)
    hits = (place8 == target).astype(f32)
    upper = (lax.broadcasted_iota(jnp.int32, (taps, taps), 0)
             < lax.broadcasted_iota(jnp.int32, (taps, taps), 1)).astype(f32).astype(bf)
    earlier = jnp.dot(hits.astype(bf), upper, preferred_element_type=f32)
    position = jnp.sum(earlier * hits, axis=0, keepdims=True).astype(jnp.int32)
    slot = target * cap + position
    group = min(512, tm * cap)
    for g in range(tm * cap // group):
        match = (slot - g * group == lax.broadcasted_iota(jnp.int32, (group, taps), 0)).astype(f32).astype(bf)
        srow[g * group : (g + 1) * group, :] = jnp.dot(
            match, tap_rows[...], preferred_element_type=f32).astype(bf)
    place = lax.broadcasted_iota(jnp.int32, (8, taps), 0)
    coded = jnp.where(place == 0, (video_of + 1).astype(f32), 0.0)
    coded = jnp.where(place == 1, (index - target * snips).astype(f32), coded).astype(bf)

    @pl.loop(0, tm)
    def _(d):
        offset = lax.rem(lax.rem(d - here + tm, tm), pack) * cap
        wide = (target - d) * 4096 + position + offset
        match = (wide == lax.broadcasted_iota(jnp.int32, (128, taps), 0)).astype(f32).astype(bf)
        sidx[d] = lax.dot_general(coded, match, (((1,), (1,)), ((), ())), preferred_element_type=f32)

    def row_copy(j):
        peer = lax.rem(here + j, tm)
        return pltpu.make_async_remote_copy(
            src_ref=srow.at[pl.ds(pl.multiple_of(peer * cap, cap), cap)], dst_ref=grow.at[j],
            send_sem=row_s.at[j], recv_sem=row_r.at[j], device_id={"tm": peer}, device_id_type=MESH)

    def idx_copy(j):
        peer = lax.rem(here + j, tm)
        return pltpu.make_async_remote_copy(
            src_ref=sidx.at[peer], dst_ref=gidx.at[j],
            send_sem=idx_s.at[j], recv_sem=idx_r.at[j], device_id={"tm": peer}, device_id_type=MESH)

    grow[0] = srow[pl.ds(pl.multiple_of(here * cap, cap), cap), :]
    gidx[0] = sidx[here]
    pl.semaphore_wait(barrier, 3 + tm - 1)

    @pl.loop(1, tm)
    def _(j):
        idx_copy(j).start()
        row_copy(j).start()

    def column_of(b, c):
        start = (b * 2 + c) * rows if aligned else c * chip
        return pl.ds(pl.multiple_of(start, 128), width)

    def lhs_copy(kind, b):
        source = (feat_ref, act)[kind]
        return pltpu.make_async_remote_copy(
            src_ref=source.at[:, column_of(b, 1 - core)],
            dst_ref=lhs.at[kind, core, :, pl.ds(b * width, width)],
            send_sem=lhs_s.at[kind, b], recv_sem=lhs_r.at[kind, b],
            device_id={"tm": sibling}, device_id_type=MESH)

    for b in range(blocks):
        lhs_copy(0, b).start()

    @pl.loop(0, own // 64)
    def _(r):
        part = pl.ds(pl.multiple_of(r * 64, 64), 64)
        values = pre_lhs_ref[part, :].astype(f32)
        act[part, :] = (values * jax.nn.sigmoid(values)).astype(bf)

    for b in range(blocks):
        lhs_copy(1, b).start()
    for side in range(2):
        at = 0 if side == 0 else snips - 1
        edge_out[side] = pack_rows(
            [row_of(ref, v * snips + at) for ref in (feat_ref, act) for v in range(videos)])
    toward = lax.rem(z + 2 * core - 1 + depth, depth)

    def edge_copy(c):
        return pltpu.make_async_remote_copy(
            src_ref=edge_out.at[core], dst_ref=edge_in.at[1 - core],
            send_sem=edge_s.at[c], recv_sem=edge_r.at[1 - core],
            device_id={"tm": toward * 2 + c}, device_id_type=MESH)

    def edge_arrival(s):
        return pltpu.make_async_remote_copy(
            src_ref=edge_out.at[0], dst_ref=edge_in.at[s],
            send_sem=edge_s.at[0], recv_sem=edge_r.at[s],
            device_id={"tm": sibling}, device_id_type=MESH)

    for c in range(2):
        edge_copy(c).start()
    for kind in range(2):
        for b in range(blocks):
            lhs[kind, core, :, b * width : (b + 1) * width] = (feat_ref, act)[kind][:, column_of(b, core)]
    for s in range(2):
        edge_arrival(s).wait_recv()
    for kind in range(2):
        for b in range(blocks):
            lhs_copy(kind, b).wait_recv()
        for b in range(blocks):
            piece = pl.ds(b * width, width)
            for v in range(videos):
                spot = kind * videos + v
                halves = [lhs[kind, c, v * snips : (v + 1) * snips, piece].astype(f32) for c in range(2)]
                ends = [jnp.where(edge_ok, edge_in[s, :, column_of(b, core)].astype(f32)[spot : spot + 1, :], 0.0)
                        for s, edge_ok in ((0, z > 0), (1, z < depth - 1))]
                for c in range(2):
                    span = pl.ds(c * own + v * snips, snips)
                    prior = ends[0] if c == 0 else halves[0][snips - 1 :, :]
                    later = ends[1] if c == 1 else halves[1][:1, :]
                    win[kind, 0, piece, span] = moved(halves[c], prior, 1).T.astype(bf)
                    win[kind, 1, piece, span] = halves[c].T.astype(bf)
                    win[kind, 2, piece, span] = moved(halves[c], later, -1).T.astype(bf)

    @pl.loop(1, tm)
    def _(j):
        idx_copy(j).wait_recv()
        row_copy(j).wait_recv()

    many = min(8, tm)
    chunk = 256
    for g in range(tm // many):
        pieces = []
        for j in range(g * many, (g + 1) * many, pack):
            both = gidx[j]
            for i in range(1, pack):
                both = both + gidx[j + i]
            code = both[0:1, :] * float(snips) + both[1:2, :] - float(snips)
            spots = lax.broadcasted_iota(jnp.int32, (own, 128), 0).astype(f32)
            pieces.append((spots == code).astype(f32).astype(bf))
        table = jnp.concatenate(pieces, axis=1)
        for n in range(cols // chunk):
            part = slice(n * chunk, (n + 1) * chunk)
            term = jnp.dot(table, grow[g * many : (g + 1) * many, :, part].reshape(many * cap, chunk),
                           preferred_element_type=f32)
            if tm == many:
                gs[core, :, part] = term.astype(bf)
            else:
                acc[:, part] = term if g == 0 else acc[:, part] + term
    if tm != many:
        gs[core] = acc[...].astype(bf)

    def grad_copy(i):
        ref = (gs, gp)[i]
        return pltpu.make_async_remote_copy(
            src_ref=ref.at[core], dst_ref=ref.at[core],
            send_sem=g_s.at[i], recv_sem=g_r.at[i], device_id={"tm": sibling}, device_id_type=MESH)

    grad_copy(0).start()
    gedge_out[...] = pack_rows([
        jnp.where(core == 1, row_of(gs, v * snips + snips - 1, core), row_of(gs, v * snips, core))
        for v in range(videos)])
    gedge_copy = pltpu.make_async_remote_copy(
        src_ref=gedge_out, dst_ref=gedge_in, send_sem=ge_s, recv_sem=ge_r,
        device_id={"tm": toward * 2 + 1 - core}, device_id_type=MESH)
    gedge_copy.start()

    def product(step):
        kind, k = (1, step) if step < 3 else (0, step - 3)
        grads = gs if step < 3 else gp

        @pl.loop(0, cols // chunk)
        def _(n):
            part = pl.ds(pl.multiple_of(n * chunk, chunk), chunk)
            q_ref[step, :, part] = jnp.dot(
                win[kind, k], grads[:, :, part].reshape(2 * own, chunk), preferred_element_type=f32).astype(bf)


    def bits(kind, xb, yb):
        return (xb, yb) if kind == 0 else (yb, xb)

    def height(step):
        return rows if step == 0 else chip

    def z_copy(j):
        peer = lax.rem(z + 1 + j, depth)
        return pltpu.make_async_remote_copy(
            src_ref=q_ref.at[0, pl.ds(z_slot_row(peer), rows)], dst_ref=rz.at[j],
            send_sem=z_s.at[j], recv_sem=z_r.at[j],
            device_id={"tm": peer * 2 + core}, device_id_type=MESH)

    def half_of(kind, h1):
        return pl.ds(pl.multiple_of(kind * (cols // 2) + h1 * half, 128), half)

    def first(step, kind):
        u = step * UNITS + kind
        h1, _ = bits(kind, 1 - x, 1 - y)
        source = zs.at[:, half_of(kind, h1)] if step == 0 else q_ref.at[step, :, half_of(kind, h1)]
        return pltpu.make_async_remote_copy(
            src_ref=source, dst_ref=r1.at[u, pl.ds(0, height(step))],
            send_sem=p1_s.at[u], recv_sem=p1_r.at[u],
            device_id={"video": (flip_x, flip_y)[kind]}, device_id_type=MESH)

    def second(step, kind):
        u = step * UNITS + kind
        _, h2 = bits(kind, 1 - x, 1 - y)
        tall = pl.ds(0, height(step))
        return pltpu.make_async_remote_copy(
            src_ref=s1.at[u, tall, pl.ds(pl.multiple_of(h2 * quarter, 128), quarter)],
            dst_ref=r2.at[u, tall],
            send_sem=p2_s.at[u], recv_sem=p2_r.at[u],
            device_id={"video": (flip_y, flip_x)[kind]}, device_id_type=MESH)

    def third(step, kind, j):
        u = step * UNITS + kind
        peer = lax.rem(z + 1 + j, depth)
        return pltpu.make_async_remote_copy(
            src_ref=t2.at[u, pl.ds(z_slot_row(peer), rows)], dst_ref=r3.at[u, j],
            send_sem=p3_s.at[u, j], recv_sem=p3_r.at[u, j],
            device_id={"tm": peer * 2 + core}, device_id_type=MESH)

    def column(kind, xb, yb):
        h1, h2 = bits(kind, xb, yb)
        return pl.ds(pl.multiple_of(kind * (cols // 2) + h1 * half + h2 * quarter, 128), quarter)

    def fourth(step, kind, j):
        u = step * UNITS + kind
        mine = out_ref.at[step, :, column(kind, x, y)]
        return pltpu.make_async_remote_copy(
            src_ref=mine, dst_ref=mine,
            send_sem=p4_s.at[u, j], recv_sem=p4_r.at[u, j],
            device_id={"video": others[j]}, device_id_type=MESH)

    def end_first(step, kind):
        u = step * UNITS + kind
        first(step, kind).wait_recv()
        h1, _ = bits(kind, x, y)
        mine = zs[:, half_of(kind, h1)] if step == 0 else q_ref[step, :, half_of(kind, h1)]
        tall = height(step)
        s1[u, :tall] = (mine.astype(f32) + r1[u, :tall].astype(f32)).astype(bf)
        second(step, kind).start()

    def second_sum(step, kind):
        u = step * UNITS + kind
        second(step, kind).wait_recv()
        _, h2 = bits(kind, x, y)
        tall = height(step)
        mine = s1[u, :tall, pl.ds(pl.multiple_of(h2 * quarter, 128), quarter)]
        return mine.astype(f32) + r2[u, :tall].astype(f32)

    def spread(step, kind, total):
        out_ref[step, :, column(kind, x, y)] = total.astype(bf)
        for j in range(3):
            fourth(step, kind, j).start()

    def end_fourth(step, kind):
        for j in range(3):
            fourth(step, kind, j).wait_recv()

    def ready(step):
        if step == 3:
            grad_copy(1).wait_recv()
        product(step)
        if step == 0:
            for j in range(depth - 1):
                z_copy(j).start()
        else:
            for kind in range(UNITS):
                first(step, kind).start()

    grad_copy(0).wait_recv()
    ready(0)
    ready(1)

    gedge_copy.wait_recv()
    outside_ok = jnp.where(core == 1, z < depth - 1, z > 0)
    outside = jnp.where(outside_ok, gedge_in[...].astype(f32), 0.0)
    for v in range(videos):
        mine = gs[core, v * snips : (v + 1) * snips, :].astype(f32)
        far = outside[v : v + 1, :]
        near = jnp.where(core == 1, row_of(gs, v * snips + snips - 1, 1 - core), row_of(gs, v * snips, 1 - core))
        prior = jnp.where(core == 1, near, far)
        later = jnp.where(core == 1, far, near)
        gmove[0, v * snips : (v + 1) * snips, :] = moved(mine, prior, 1).astype(bf)
        gmove[1, v * snips : (v + 1) * snips, :] = moved(mine, later, -1).astype(bf)
    filt_copy.wait()

    @pl.loop(0, cols // chunk)
    def _(n):
        part = pl.ds(pl.multiple_of(n * chunk, chunk), chunk)
        total = jnp.zeros((own, chunk), f32)
        for lag, window in enumerate((gmove[1], gs[core], gmove[0])):
            total = total + lax.dot_general(
                window, filt[lag, part, :], (((1,), (1,)), ((), ())), preferred_element_type=f32)
        gp[core, :, part] = (total * silu_slope(pre_ref[:, part].astype(f32))).astype(bf)

    grad_copy(1).start()
    ready(2)


    kinds = range(UNITS)
    for turn in range(steps + 2):
        if turn + 3 < steps:
            ready(turn + 3)
        if turn == 2:
            total = q_ref[0, pl.ds(z_slot_row(z), rows)].astype(f32)
            for j in range(depth - 1):
                z_copy(j).wait_recv()
                total = total + rz[j].astype(f32)
            zs[...] = total.astype(bf)
            for kind in kinds:
                first(0, kind).start()
        if turn == 3:
            for kind in kinds:
                end_first(0, kind)
        if turn == 4:
            for kind in kinds:
                spread(0, kind, second_sum(0, kind))
        if turn == 5:
            for kind in kinds:
                end_fourth(0, kind)
        step = turn + 1
        if 1 <= step < steps:
            for kind in kinds:
                end_first(step, kind)
        step = turn
        if 1 <= step < steps:
            for kind in kinds:
                t2[step * UNITS + kind] = second_sum(step, kind).astype(bf)
                for j in range(depth - 1):
                    third(step, kind, j).start()
        step = turn - 1
        if 1 <= step < steps:
            for kind in kinds:
                u = step * UNITS + kind
                total = t2[u, pl.ds(z_slot_row(z), rows)].astype(f32)
                for j in range(depth - 1):
                    third(step, kind, j).wait_recv()
                    total = total + r3[u, j].astype(f32)
                spread(step, kind, total)
        step = turn - 2
        if 1 <= step < steps:
            for kind in kinds:
                end_fourth(step, kind)

    for j in range(depth - 1):
        z_copy(j).wait_send()
    for step in range(steps):
        for kind in kinds:
            first(step, kind).wait_send()
            second(step, kind).wait_send()
            for j in range(depth - 1):
                if step > 0:
                    third(step, kind, j).wait_send()
            for j in range(3):
                fourth(step, kind, j).wait_send()
    for c in range(2):
        edge_copy(c).wait_send()
    for kind in range(2):
        for b in range(blocks):
            lhs_copy(kind, b).wait_send()
    for i in range(2):
        grad_copy(i).wait_send()
    gedge_copy.wait_send()

    @pl.loop(1, tm)
    def _(j):
        idx_copy(j).wait_send()
        row_copy(j).wait_send()


def on_device(bin_grad, tap_weight, tap_index, features, preact, filter_second):
    video_count, prop_count, bin_count, tap_count = tap_index.shape
    snips, cols = features.shape[1:]
    tm = lax.axis_size("tm")
    depth = tm // 2
    rows = cols // tm
    chip = depth * rows
    own = video_count * snips
    bins = video_count * prop_count * bin_count
    cap = bin_count * tap_count * ((video_count * prop_count + tm - 1) // tm)
    steps = 6
    n = steps * UNITS
    half, quarter = cols // 4, cols // 8
    blocks = depth if rows % 128 == 0 else 1
    bf, f32 = jnp.bfloat16, jnp.float32
    dma = pltpu.SemaphoreType.DMA
    vmem = pl.BlockSpec(memory_space=pltpu.VMEM)
    features = features.reshape(own, cols)
    preact = preact.reshape(own, cols)

    def by_core(values):
        if rows % 128 == 0:
            return values
        return values.reshape(own, depth, 2, rows).swapaxes(1, 2).reshape(own, cols)

    aligned = rows % 128 == 0
    sizes = (tm, steps, rows, cols, video_count, snips, cap)

    def kernel(bin_ref, weight_ref, index_ref, feat_ref, pre_ref, *refs):
        lhs_refs = (pre_ref,) if aligned else ()
        whole_kernel(*sizes, bin_ref, weight_ref, index_ref, feat_ref, pre_ref, *lhs_refs, *refs)

    sums = pl.pallas_call(
        kernel,
        out_shape=jax.ShapeDtypeStruct((steps, rows, cols), bf),
        in_specs=[vmem] * (5 if aligned else 6) + [pl.BlockSpec(memory_space=pl.ANY)],
        out_specs=vmem,
        scratch_shapes=[
            pltpu.VMEM(filter_second.shape, bf),
            pltpu.VMEM((2 * bins, cols), bf),
            pltpu.VMEM((tm * cap, cols), bf),
            pltpu.VMEM((tm, 8, 128), f32),
            pltpu.VMEM((tm, cap, cols), bf),
            pltpu.VMEM((tm, 8, 128), f32),
            pltpu.VMEM((own, cols), bf),
            pltpu.VMEM((2, 2, own, chip), bf),
            pltpu.VMEM((2, 3, chip, 2 * own), bf),
            pltpu.VMEM((2, 16, cols), bf),
            pltpu.VMEM((2, 16, cols), bf),
            pltpu.VMEM((2, own, cols), bf),
            pltpu.VMEM((2, own, cols), bf),
            pltpu.VMEM((2, own, cols), bf),
            pltpu.VMEM((16, cols), bf),
            pltpu.VMEM((16, cols), bf),
            pltpu.VMEM((own, cols) if tm > 8 else (8, 128), f32),
            pltpu.VMEM((steps, chip, cols), bf),
            pltpu.VMEM((n, chip, half), bf),
            pltpu.VMEM((n, chip, half), bf),
            pltpu.VMEM((n, chip, quarter), bf),
            pltpu.VMEM((n, chip, quarter), bf),
            pltpu.VMEM((n, depth - 1, rows, quarter), bf),
            pltpu.VMEM((depth - 1, rows, cols), bf),
            pltpu.VMEM((rows, cols), bf),
            dma((depth - 1,)), dma((depth - 1,)),
            dma((n,)), dma((n,)), dma((n,)), dma((n,)),
            dma((n, depth - 1)), dma((n, depth - 1)), dma((n, 3)), dma((n, 3)),
            dma((tm,)), dma((tm,)), dma((tm,)), dma((tm,)),
            dma((2, blocks)), dma((2, blocks)), dma((2,)), dma((2,)),
            dma((2,)), dma((2,)), dma, dma, dma,
        ],
        compiler_params=pltpu.CompilerParams(
            collective_id=0, has_side_effects=True, vmem_limit_bytes=VMEM_LIMIT
        ),
        name="filter_grads",
    )(
        bin_grad.reshape(bins, cols),
        tap_weight.reshape(bins, tap_count),
        tap_index.reshape(bins, tap_count).T.reshape(1, tap_count * bins),
        by_core(features),
        preact,
        *(() if aligned else (by_core(preact),)),
        filter_second,
    )
    out = sums.astype(f32).reshape(2, 3, rows, cols).transpose(0, 2, 1, 3)
    return (out[1], out[0])


def solution(mesh):
    return jax.shard_map(
        on_device,
        mesh=mesh,
        in_specs=(
            P("video", "tm", None, None),
            P("video", "tm", None, None),
            P("video", "tm", None, None),
            P("video", "tm", None),
            P("video", "tm", None),
            P(),
        ),
        out_specs=(P("tm", None, None), P("tm", None, None)),
        check_vma=False,
    )
```

```python
import functools

import jax
import jax.numpy as jnp
from jax import lax
from jax.experimental import pallas as pl
from jax.experimental.pallas import tpu as pltpu
from jax.sharding import PartitionSpec as P

MESH = pl.DeviceIdType.MESH
UNITS = 2
VMEM_LIMIT = 60 * 1024 * 1024


def silu_slope(values):
    sigma = jax.nn.sigmoid(values)
    return sigma * (1.0 + values * (1.0 - sigma))


def row_of(ref, index, *lead):
    group = ref[(*lead, pl.ds(index // 16 * 16, 16), slice(None))].astype(jnp.float32)
    return group[index % 16 : index % 16 + 1, :]


def pack_rows(row_list):
    width = row_list[0].shape[1]
    place = lax.broadcasted_iota(jnp.int32, (16, width), 0)
    packed = jnp.zeros((16, width), jnp.float32)
    for i, row in enumerate(row_list):
        packed = jnp.where(place == i, row, packed)
    return packed.astype(jnp.bfloat16)


def moved(block, edge, amount):
    count = block.shape[0]
    place = lax.broadcasted_iota(jnp.int32, block.shape, 0)
    if amount == 1:
        return jnp.where(place == 0, edge, pltpu.roll(block, 1, 0))
    return jnp.where(place == count - 1, edge, pltpu.roll(block, count - 1, 0))


def whole_kernel(tm, steps, rows, cols, videos, snips, cap, bin_ref, weight_ref, index_ref, feat_ref,
                 pre_ref, pre_lhs_ref, filt_hbm, out_ref, filt, tap_rows, srow, sidx, grow, gidx, lhs, win,
                 edge_out, edge_in, gs, gp, gmove, gedge_out, gedge_in, acc, q_ref,
                 r1, s1, r2, t2, r3, rz, zs, z_s, z_r,
                 p1_s, p1_r, p2_s, p2_r, p3_s, p3_r, p4_s, p4_r,
                 row_s, row_r, idx_s, idx_r, lhs_s, lhs_r, edge_s, edge_r, g_s, g_r, ge_s, ge_r, filt_sem):
    depth = tm // 2
    bf, f32 = jnp.bfloat16, jnp.float32
    own = videos * snips
    bins = bin_ref.shape[0]
    taps = 2 * bins
    chip = depth * rows
    aligned = rows % 128 == 0
    pack = 128 // cap
    blocks = depth if aligned else 1
    width = chip // blocks
    video = lax.axis_index("video")
    here = lax.axis_index("tm")
    x, y = lax.rem(video, 2), video // 2
    core, z = lax.rem(here, 2), here // 2
    sibling = z * 2 + 1 - core
    flip_x = y * 2 + (1 - x)
    flip_y = (1 - y) * 2 + x
    flip_xy = (1 - y) * 2 + (1 - x)
    others = (flip_x, flip_y, flip_xy)
    half, quarter = cols // 4, cols // 8

    def z_slot_row(peer_z):
        return pl.multiple_of(peer_z * rows, rows)

    filt_copy = pltpu.make_async_copy(filt_hbm, filt, filt_sem)
    filt_copy.start()
    barrier = pltpu.get_barrier_semaphore()
    for v in others:
        pl.semaphore_signal(barrier, inc=1, device_id={"video": v}, device_id_type=MESH)

    @pl.loop(1, tm)
    def _(j):
        pl.semaphore_signal(barrier, inc=1, device_id={"tm": lax.rem(here + j, tm)}, device_id_type=MESH)

    inputs = (feat_ref, pre_lhs_ref)

    def column_of(b, c):
        start = (b * 2 + c) * rows if aligned else c * chip
        return pl.ds(pl.multiple_of(start, 128), width)

    def lhs_copy(kind, b):
        source = inputs[kind]
        return pltpu.make_async_remote_copy(
            src_ref=source.at[:, column_of(b, 1 - core)],
            dst_ref=lhs.at[kind, core, :, pl.ds(b * width, width)],
            send_sem=lhs_s.at[kind, b], recv_sem=lhs_r.at[kind, b],
            device_id={"tm": sibling}, device_id_type=MESH)

    for side in range(2):
        at = 0 if side == 0 else snips - 1
        edge_out[side] = pack_rows(
            [row_of(ref, v * snips + at) for ref in inputs for v in range(videos)])
    toward = lax.rem(z + 2 * core - 1 + depth, depth)

    def edge_copy(c):
        return pltpu.make_async_remote_copy(
            src_ref=edge_out.at[core], dst_ref=edge_in.at[1 - core],
            send_sem=edge_s.at[c], recv_sem=edge_r.at[1 - core],
            device_id={"tm": toward * 2 + c}, device_id_type=MESH)

    def edge_arrival(s):
        return pltpu.make_async_remote_copy(
            src_ref=edge_out.at[0], dst_ref=edge_in.at[s],
            send_sem=edge_s.at[0], recv_sem=edge_r.at[s],
            device_id={"tm": sibling}, device_id_type=MESH)

    pl.semaphore_wait(barrier, 3 + tm - 1)
    for c in range(2):
        edge_copy(c).start()
    for kind in range(2):
        for b in range(blocks):
            lhs_copy(kind, b).start()

    for j in range(2):
        tap_rows[j * bins : (j + 1) * bins, :] = (
            weight_ref[:, j : j + 1] * bin_ref[...].astype(f32)).astype(bf)
    index = index_ref[...]
    target = index // snips
    lane = lax.broadcasted_iota(jnp.int32, (1, taps), 1)
    video_of = lax.rem(lane, bins) // (bins // videos)
    place8 = lax.broadcasted_iota(jnp.int32, (tm, taps), 0)
    hits = (place8 == target).astype(f32)
    upper = (lax.broadcasted_iota(jnp.int32, (taps, taps), 0)
             < lax.broadcasted_iota(jnp.int32, (taps, taps), 1)).astype(f32).astype(bf)
    earlier = jnp.dot(hits.astype(bf), upper, preferred_element_type=f32)
    position = jnp.sum(earlier * hits, axis=0, keepdims=True).astype(jnp.int32)
    slot = target * cap + position
    group = min(512, tm * cap)
    for g in range(tm * cap // group):
        match = (slot - g * group == lax.broadcasted_iota(jnp.int32, (group, taps), 0)).astype(f32).astype(bf)
        srow[g * group : (g + 1) * group, :] = jnp.dot(
            match, tap_rows[...], preferred_element_type=f32).astype(bf)
    place = lax.broadcasted_iota(jnp.int32, (8, taps), 0)
    coded = jnp.where(place == 0, (video_of + 1).astype(f32), 0.0)
    coded = jnp.where(place == 1, (index - target * snips).astype(f32), coded).astype(bf)

    @pl.loop(0, tm)
    def _(d):
        offset = lax.rem(lax.rem(d - here + tm, tm), pack) * cap
        wide = (target - d) * 4096 + position + offset
        match = (wide == lax.broadcasted_iota(jnp.int32, (128, taps), 0)).astype(f32).astype(bf)
        sidx[d] = lax.dot_general(coded, match, (((1,), (1,)), ((), ())), preferred_element_type=f32)

    def row_copy(j):
        peer = lax.rem(here + j, tm)
        return pltpu.make_async_remote_copy(
            src_ref=srow.at[pl.ds(pl.multiple_of(peer * cap, cap), cap)], dst_ref=grow.at[j],
            send_sem=row_s.at[j], recv_sem=row_r.at[j], device_id={"tm": peer}, device_id_type=MESH)

    def idx_copy(j):
        peer = lax.rem(here + j, tm)
        return pltpu.make_async_remote_copy(
            src_ref=sidx.at[peer], dst_ref=gidx.at[j],
            send_sem=idx_s.at[j], recv_sem=idx_r.at[j], device_id={"tm": peer}, device_id_type=MESH)

    grow[0] = srow[pl.ds(pl.multiple_of(here * cap, cap), cap), :]
    gidx[0] = sidx[here]

    @pl.loop(1, tm)
    def _(i):
        j = lax.rem(i - 1 + tm // 2 - 1, tm - 1) + 1
        idx_copy(j).start()
        row_copy(j).start()

    for kind in range(2):
        for b in range(blocks):
            lhs[kind, core, :, b * width : (b + 1) * width] = inputs[kind][:, column_of(b, core)]
    shape_of = (lambda values: values, lambda values: values * jax.nn.sigmoid(values))
    for s in range(2):
        edge_arrival(s).wait_recv()
    for kind in range(2):
        for b in range(blocks):
            lhs_copy(kind, b).wait_recv()
        for b in range(blocks):
            piece = pl.ds(b * width, width)
            for v in range(videos):
                spot = kind * videos + v
                halves = [shape_of[kind](lhs[kind, c, v * snips : (v + 1) * snips, piece].astype(f32))
                          for c in range(2)]
                ends = [jnp.where(edge_ok, shape_of[kind](
                            edge_in[s, :, column_of(b, core)].astype(f32)[spot : spot + 1, :]), 0.0)
                        for s, edge_ok in ((0, z > 0), (1, z < depth - 1))]
                for c in range(2):
                    span = pl.ds(c * own + v * snips, snips)
                    prior = ends[0] if c == 0 else halves[0][snips - 1 :, :]
                    later = ends[1] if c == 1 else halves[1][:1, :]
                    win[kind, 0, piece, span] = moved(halves[c], prior, 1).T.astype(bf)
                    win[kind, 1, piece, span] = halves[c].T.astype(bf)
                    win[kind, 2, piece, span] = moved(halves[c], later, -1).T.astype(bf)

    @pl.loop(1, tm)
    def _(j):
        idx_copy(j).wait_recv()
        row_copy(j).wait_recv()

    many = min(8, tm)
    chunk = 256
    for g in range(tm // many):
        pieces = []
        for j in range(g * many, (g + 1) * many, pack):
            both = gidx[j]
            for i in range(1, pack):
                both = both + gidx[j + i]
            code = both[0:1, :] * float(snips) + both[1:2, :] - float(snips)
            spots = lax.broadcasted_iota(jnp.int32, (own, 128), 0).astype(f32)
            pieces.append((spots == code).astype(f32).astype(bf))
        table = jnp.concatenate(pieces, axis=1)
        for n in range(cols // chunk):
            part = slice(n * chunk, (n + 1) * chunk)
            term = jnp.dot(table, grow[g * many : (g + 1) * many, :, part].reshape(many * cap, chunk),
                           preferred_element_type=f32)
            if tm == many:
                gs[core, :, part] = term.astype(bf)
            else:
                acc[:, part] = term if g == 0 else acc[:, part] + term
    if tm != many:
        gs[core] = acc[...].astype(bf)

    def grad_copy(i):
        ref = (gs, gp)[i]
        return pltpu.make_async_remote_copy(
            src_ref=ref.at[core], dst_ref=ref.at[core],
            send_sem=g_s.at[i], recv_sem=g_r.at[i], device_id={"tm": sibling}, device_id_type=MESH)

    grad_copy(0).start()
    gedge_out[...] = pack_rows([
        jnp.where(core == 1, row_of(gs, v * snips + snips - 1, core), row_of(gs, v * snips, core))
        for v in range(videos)])
    gedge_copy = pltpu.make_async_remote_copy(
        src_ref=gedge_out, dst_ref=gedge_in, send_sem=ge_s, recv_sem=ge_r,
        device_id={"tm": toward * 2 + 1 - core}, device_id_type=MESH)
    gedge_copy.start()

    def product(step):
        kind, k = (1, step) if step < 3 else (0, step - 3)
        grads = gs if step < 3 else gp

        @pl.loop(0, cols // chunk)
        def _(n):
            part = pl.ds(pl.multiple_of(n * chunk, chunk), chunk)
            q_ref[step, :, part] = jnp.dot(
                win[kind, k], grads[:, :, part].reshape(2 * own, chunk), preferred_element_type=f32).astype(bf)


    def bits(kind, xb, yb):
        return (xb, yb) if kind == 0 else (yb, xb)

    def height(step):
        return rows if step == 0 else chip

    def z_copy(j):
        peer = lax.rem(z + 1 + j, depth)
        return pltpu.make_async_remote_copy(
            src_ref=q_ref.at[0, pl.ds(z_slot_row(peer), rows)], dst_ref=rz.at[j],
            send_sem=z_s.at[j], recv_sem=z_r.at[j],
            device_id={"tm": peer * 2 + core}, device_id_type=MESH)

    def half_of(kind, h1):
        return pl.ds(pl.multiple_of(kind * (cols // 2) + h1 * half, 128), half)

    def first(step, kind):
        u = step * UNITS + kind
        h1, _ = bits(kind, 1 - x, 1 - y)
        source = zs.at[:, half_of(kind, h1)] if step == 0 else q_ref.at[step, :, half_of(kind, h1)]
        return pltpu.make_async_remote_copy(
            src_ref=source, dst_ref=r1.at[u, pl.ds(0, height(step))],
            send_sem=p1_s.at[u], recv_sem=p1_r.at[u],
            device_id={"video": (flip_x, flip_y)[kind]}, device_id_type=MESH)

    def second(step, kind):
        u = step * UNITS + kind
        _, h2 = bits(kind, 1 - x, 1 - y)
        tall = pl.ds(0, height(step))
        return pltpu.make_async_remote_copy(
            src_ref=s1.at[u, tall, pl.ds(pl.multiple_of(h2 * quarter, 128), quarter)],
            dst_ref=r2.at[u, tall],
            send_sem=p2_s.at[u], recv_sem=p2_r.at[u],
            device_id={"video": (flip_y, flip_x)[kind]}, device_id_type=MESH)

    def third(step, kind, j):
        u = step * UNITS + kind
        peer = lax.rem(z + 1 + j, depth)
        return pltpu.make_async_remote_copy(
            src_ref=t2.at[u, pl.ds(z_slot_row(peer), rows)], dst_ref=r3.at[u, j],
            send_sem=p3_s.at[u, j], recv_sem=p3_r.at[u, j],
            device_id={"tm": peer * 2 + core}, device_id_type=MESH)

    def column(kind, xb, yb):
        h1, h2 = bits(kind, xb, yb)
        return pl.ds(pl.multiple_of(kind * (cols // 2) + h1 * half + h2 * quarter, 128), quarter)

    def fourth(step, kind, j):
        u = step * UNITS + kind
        mine = out_ref.at[step, :, column(kind, x, y)]
        return pltpu.make_async_remote_copy(
            src_ref=mine, dst_ref=mine,
            send_sem=p4_s.at[u, j], recv_sem=p4_r.at[u, j],
            device_id={"video": others[j]}, device_id_type=MESH)

    def end_first(step, kind):
        u = step * UNITS + kind
        first(step, kind).wait_recv()
        h1, _ = bits(kind, x, y)
        mine = zs[:, half_of(kind, h1)] if step == 0 else q_ref[step, :, half_of(kind, h1)]
        tall = height(step)
        s1[u, :tall] = (mine.astype(f32) + r1[u, :tall].astype(f32)).astype(bf)
        second(step, kind).start()

    def second_sum(step, kind):
        u = step * UNITS + kind
        second(step, kind).wait_recv()
        _, h2 = bits(kind, x, y)
        tall = height(step)
        mine = s1[u, :tall, pl.ds(pl.multiple_of(h2 * quarter, 128), quarter)]
        return mine.astype(f32) + r2[u, :tall].astype(f32)

    def spread(step, kind, total):
        out_ref[step, :, column(kind, x, y)] = total.astype(bf)
        for j in range(3):
            fourth(step, kind, j).start()

    def end_fourth(step, kind):
        for j in range(3):
            fourth(step, kind, j).wait_recv()

    def ready(step):
        if step == 3:
            grad_copy(1).wait_recv()
        product(step)
        if step == 0:
            for j in range(depth - 1):
                z_copy(j).start()
        else:
            for kind in range(UNITS):
                first(step, kind).start()

    grad_copy(0).wait_recv()
    ready(0)
    ready(1)

    gedge_copy.wait_recv()
    outside_ok = jnp.where(core == 1, z < depth - 1, z > 0)
    outside = jnp.where(outside_ok, gedge_in[...].astype(f32), 0.0)
    for v in range(videos):
        mine = gs[core, v * snips : (v + 1) * snips, :].astype(f32)
        far = outside[v : v + 1, :]
        near = jnp.where(core == 1, row_of(gs, v * snips + snips - 1, 1 - core), row_of(gs, v * snips, 1 - core))
        prior = jnp.where(core == 1, near, far)
        later = jnp.where(core == 1, far, near)
        gmove[0, v * snips : (v + 1) * snips, :] = moved(mine, prior, 1).astype(bf)
        gmove[1, v * snips : (v + 1) * snips, :] = moved(mine, later, -1).astype(bf)
    filt_copy.wait()

    @pl.loop(0, cols // chunk)
    def _(n):
        part = pl.ds(pl.multiple_of(n * chunk, chunk), chunk)
        total = jnp.zeros((own, chunk), f32)
        for lag, window in enumerate((gmove[1], gs[core], gmove[0])):
            total = total + lax.dot_general(
                window, filt[lag, part, :], (((1,), (1,)), ((), ())), preferred_element_type=f32)
        gp[core, :, part] = (total * silu_slope(pre_ref[:, part].astype(f32))).astype(bf)

    grad_copy(1).start()
    ready(2)


    kinds = range(UNITS)
    for turn in range(steps + 2):
        if turn + 3 < steps:
            ready(turn + 3)
        if turn == 3:
            total = q_ref[0, pl.ds(z_slot_row(z), rows)].astype(f32)
            for j in range(depth - 1):
                z_copy(j).wait_recv()
                total = total + rz[j].astype(f32)
            zs[...] = total.astype(bf)
            for kind in kinds:
                first(0, kind).start()
        if turn == 4:
            for kind in kinds:
                end_first(0, kind)
        if turn == 5:
            for kind in kinds:
                spread(0, kind, second_sum(0, kind))
        if turn == 6:
            for kind in kinds:
                end_fourth(0, kind)
        step = turn + 1
        if 1 <= step < steps:
            for kind in kinds:
                end_first(step, kind)
        step = turn
        if 1 <= step < steps:
            for kind in kinds:
                t2[step * UNITS + kind] = second_sum(step, kind).astype(bf)
                for j in range(depth - 1):
                    third(step, kind, j).start()
        step = turn - 1
        if 1 <= step < steps:
            for kind in kinds:
                u = step * UNITS + kind
                total = t2[u, pl.ds(z_slot_row(z), rows)].astype(f32)
                for j in range(depth - 1):
                    third(step, kind, j).wait_recv()
                    total = total + r3[u, j].astype(f32)
                spread(step, kind, total)
        step = turn - 2
        if 1 <= step < steps:
            for kind in kinds:
                end_fourth(step, kind)

    for j in range(depth - 1):
        z_copy(j).wait_send()
    for step in range(steps):
        for kind in kinds:
            first(step, kind).wait_send()
            second(step, kind).wait_send()
            for j in range(depth - 1):
                if step > 0:
                    third(step, kind, j).wait_send()
            for j in range(3):
                fourth(step, kind, j).wait_send()
    for c in range(2):
        edge_copy(c).wait_send()
    for kind in range(2):
        for b in range(blocks):
            lhs_copy(kind, b).wait_send()
    for i in range(2):
        grad_copy(i).wait_send()
    gedge_copy.wait_send()

    @pl.loop(1, tm)
    def _(j):
        idx_copy(j).wait_send()
        row_copy(j).wait_send()


def on_device(bin_grad, tap_weight, tap_index, features, preact, filter_second):
    video_count, prop_count, bin_count, tap_count = tap_index.shape
    snips, cols = features.shape[1:]
    tm = lax.axis_size("tm")
    depth = tm // 2
    rows = cols // tm
    chip = depth * rows
    own = video_count * snips
    bins = video_count * prop_count * bin_count
    cap = bin_count * tap_count * ((video_count * prop_count + tm - 1) // tm)
    steps = 6
    n = steps * UNITS
    half, quarter = cols // 4, cols // 8
    blocks = depth if rows % 128 == 0 else 1
    bf, f32 = jnp.bfloat16, jnp.float32
    dma = pltpu.SemaphoreType.DMA
    vmem = pl.BlockSpec(memory_space=pltpu.VMEM)
    features = features.reshape(own, cols)
    preact = preact.reshape(own, cols)

    def by_core(values):
        if rows % 128 == 0:
            return values
        return values.reshape(own, depth, 2, rows).swapaxes(1, 2).reshape(own, cols)

    aligned = rows % 128 == 0
    sizes = (tm, steps, rows, cols, video_count, snips, cap)

    def kernel(bin_ref, weight_ref, index_ref, feat_ref, pre_ref, *refs):
        lhs_refs = (pre_ref,) if aligned else ()
        whole_kernel(*sizes, bin_ref, weight_ref, index_ref, feat_ref, pre_ref, *lhs_refs, *refs)

    sums = pl.pallas_call(
        kernel,
        out_shape=jax.ShapeDtypeStruct((steps, rows, cols), bf),
        in_specs=[vmem] * (5 if aligned else 6) + [pl.BlockSpec(memory_space=pl.ANY)],
        out_specs=vmem,
        scratch_shapes=[
            pltpu.VMEM(filter_second.shape, bf),
            pltpu.VMEM((2 * bins, cols), bf),
            pltpu.VMEM((tm * cap, cols), bf),
            pltpu.VMEM((tm, 8, 128), f32),
            pltpu.VMEM((tm, cap, cols), bf),
            pltpu.VMEM((tm, 8, 128), f32),
            pltpu.VMEM((2, 2, own, chip), bf),
            pltpu.VMEM((2, 3, chip, 2 * own), bf),
            pltpu.VMEM((2, 16, cols), bf),
            pltpu.VMEM((2, 16, cols), bf),
            pltpu.VMEM((2, own, cols), bf),
            pltpu.VMEM((2, own, cols), bf),
            pltpu.VMEM((2, own, cols), bf),
            pltpu.VMEM((16, cols), bf),
            pltpu.VMEM((16, cols), bf),
            pltpu.VMEM((own, cols) if tm > 8 else (8, 128), f32),
            pltpu.VMEM((steps, chip, cols), bf),
            pltpu.VMEM((n, chip, half), bf),
            pltpu.VMEM((n, chip, half), bf),
            pltpu.VMEM((n, chip, quarter), bf),
            pltpu.VMEM((n, chip, quarter), bf),
            pltpu.VMEM((n, depth - 1, rows, quarter), bf),
            pltpu.VMEM((depth - 1, rows, cols), bf),
            pltpu.VMEM((rows, cols), bf),
            dma((depth - 1,)), dma((depth - 1,)),
            dma((n,)), dma((n,)), dma((n,)), dma((n,)),
            dma((n, depth - 1)), dma((n, depth - 1)), dma((n, 3)), dma((n, 3)),
            dma((tm,)), dma((tm,)), dma((tm,)), dma((tm,)),
            dma((2, blocks)), dma((2, blocks)), dma((2,)), dma((2,)),
            dma((2,)), dma((2,)), dma, dma, dma,
        ],
        compiler_params=pltpu.CompilerParams(
            collective_id=0, has_side_effects=True, vmem_limit_bytes=VMEM_LIMIT
        ),
        name="filter_grads",
    )(
        bin_grad.reshape(bins, cols),
        tap_weight.reshape(bins, tap_count),
        tap_index.reshape(bins, tap_count).T.reshape(1, tap_count * bins),
        by_core(features),
        preact,
        *(() if aligned else (by_core(preact),)),
        filter_second,
    )
    out = sums.astype(f32).reshape(2, 3, rows, cols).transpose(0, 2, 1, 3)
    return (out[1], out[0])


def solution(mesh):
    return jax.shard_map(
        on_device,
        mesh=mesh,
        in_specs=(
            P("video", "tm", None, None),
            P("video", "tm", None, None),
            P("video", "tm", None, None),
            P("video", "tm", None),
            P("video", "tm", None),
            P(),
        ),
        out_specs=(P("tm", None, None), P("tm", None, None)),
        check_vma=False,
    )
```
